32 devices in a mesh: grp: 2 (over x), cell: 16 (over z, y, core).
Axes of the slice: x: 2, y: 2, z: 4, core: 2. Of those that a mesh axis runs over, the one named last changes fastest.
Arguments:
- counts: bfloat16 [65536, 2560], P(('grp', 'cell')), parts along dimension 0, may hold values from 0.0099487305 to 4
- cell_init: float32 [64, 65536], P(None, ('grp', 'cell')), parts along dimension 1, may hold values from 0.1 to 1
- load_init: float32 [64, 5120], P(None, ('grp', 'cell')), parts along dimension 1, may hold values from 0.1 to 1
- band_offsets: int32 [512, 3], P(('grp', 'cell')), parts along dimension 0, may hold values from -2 to 2
- band_weights: bfloat16 [512, 3, 128, 128], P(('grp', 'cell')), parts along dimension 0, may hold values from 0.049804688 to 1
Outputs:
- cell_factors: float32 [64, 65536], P(None, ('grp', 'cell')), parts along dimension 1
- gene_loadings: float32 [64, 5120], P(None, ('grp', 'cell')), parts along dimension 1
- fit_error: float32 [65536], P(('grp', 'cell')), parts along dimension 0
The draws below stay inside these ranges and needn't reach their ends.
There are 2 independent parts, one for each index of `grp`. The reference program is written for one: setup_inputs(seed, part) draws one part's arguments, and reference() takes and returns one part's arrays. A program takes and returns all parts, laid end to end along the dimension named above; each array names one. Nothing has to cross between parts.
Inputs may be any that keep to these rules, and one draw needn't show every extreme that they name: `band_offsets`: cell block b couples to cell block b plus this offset; blocks outside the slab hold zero factors.
All inputs are finite; a program needn't handle non-finite values.
Results may differ from the reference program's by a relative error of at most 0.0003.
Values may be sent and summed in bfloat16 or wider, within the bound.
A program may use at most 64 MiB of HBM per device.

```python
import math
import jax
import jax.numpy as jnp
from jax import lax

RANK = 64
G = 2560
BLOCK = 128
SLOTS = 3
ITERS = 2
CELLS = 32768
BLOCKS = 256


def plant(entries, stream_key, smallest, top_value):
    extent = entries.shape
    index_at = [jax.random.randint(jax.random.fold_in(stream_key, axis), (), 0, extent[axis]) for axis in range(len(extent))]
    entries = entries.at[tuple(index_at)].set(smallest)
    longest = extent.index(max(extent))
    index_at[longest] = (index_at[longest] + 1) % extent[longest]
    return entries.at[tuple(index_at)].set(top_value)


def block_levels(own_key, extent, shards, low, largest):
    loudness = 1.0
    for axis_at, shards_of in shards:
        steps = jax.random.uniform(jax.random.fold_in(jax.random.fold_in(own_key, 6), axis_at), (shards_of,), jnp.float32, low / len(shards), largest / len(shards))
        loudness = loudness * jnp.repeat(jnp.exp(steps), extent[axis_at] // shards_of).reshape((-1,) + (1,) * (len(extent) - 1 - axis_at))
    return loudness


def setup_inputs(seed: int = 0, part: int = 0) -> dict:
    keys = jax.random.split(jax.random.key(seed), 6)
    own_keys = jax.random.split(jax.random.fold_in(keys[5], part), 6)
    return {
        "counts": jnp.clip(jnp.exp(math.log(4.0) - 5.996605 * jax.random.uniform(own_keys[0], (CELLS, G), jnp.float32) ** block_levels(own_keys[0], (CELLS, G), ((0, 16),), -0.2, 0.2)), 0.0099487305, 4.0).astype(jnp.bfloat16),
        "cell_init": jnp.clip(0.1 + 0.9 * jax.random.uniform(own_keys[1], (RANK, CELLS), jnp.float32) ** block_levels(own_keys[1], (RANK, CELLS), ((1, 16),), -0.2, 0.2), 0.1, 1.0),
        "load_init": jnp.clip(0.1 + 0.9 * jax.random.uniform(own_keys[2], (RANK, G), jnp.float32) ** block_levels(own_keys[2], (RANK, G), ((1, 16),), -0.2, 0.2), 0.1, 1.0),
        "band_offsets": plant(jax.random.randint(own_keys[3], (BLOCKS, SLOTS), -2, 3), jax.random.fold_in(own_keys[3], 1), -2, 2).astype(jnp.int32),
        "band_weights": jnp.clip(0.049804688 + 0.9501953 * jax.random.uniform(own_keys[4], (BLOCKS, SLOTS, BLOCK, BLOCK), jnp.float32) ** block_levels(own_keys[4], (BLOCKS, SLOTS, BLOCK, BLOCK), ((0, 16),), -0.2, 0.2), 0.049804688, 1.0).astype(jnp.bfloat16),
    }


graph_weight = 0.5
epsilon = 1e-9


def graph_product(fact_half, band_offsets, band_weights):
    rank = fact_half.shape[0]
    nblocks = band_weights.shape[0]
    block = band_weights.shape[-1]
    padded = jnp.pad(fact_half, ((0, 0), (2 * block, 2 * block)))
    blocks = padded.reshape(rank, nblocks + 4, block)
    positions = (jnp.arange(nblocks, dtype=jnp.int32)[:, None] + 2 + band_offsets).astype(jnp.int32)
    picked = jnp.take(blocks, positions, axis=1)
    result = jnp.einsum("nsij,knsj->kni", band_weights.astype(jnp.float32), picked.astype(jnp.float32))
    return result.reshape(rank, nblocks * block)


def reference(counts, cell_init, load_init, band_offsets, band_weights):
    highest = lax.Precision.HIGHEST
    factors = cell_init
    loadings = load_init
    degree = jnp.sum(band_weights.astype(jnp.float32), axis=(1, 3)).reshape(-1)
    load_half = loadings.astype(jnp.bfloat16)
    for sweep in range(ITERS):
        fact_half = factors.astype(jnp.bfloat16)
        cross_sums = jnp.dot(fact_half, counts, preferred_element_type=jnp.float32)
        factor_gram = jnp.dot(factors, factors.T, precision=highest)
        loadings = loadings * cross_sums / (jnp.dot(factor_gram, loadings, precision=highest) + epsilon)
        load_half = loadings.astype(jnp.bfloat16)
        load_gram = jnp.dot(loadings, loadings.T, precision=highest)
        data_term = lax.dot_general(load_half, counts, (((1,), (1,)), ((), ())), preferred_element_type=jnp.float32)
        graph_term = graph_product(fact_half, band_offsets, band_weights)
        numer = data_term + graph_weight * graph_term
        denom = jnp.dot(load_gram, factors, precision=highest) + graph_weight * degree[None, :] * factors + epsilon
        factors = factors * numer / denom
    fact_half = factors.astype(jnp.bfloat16)
    rows_total = counts.shape[0]
    count_blocks = counts.reshape(rows_total // BLOCK, BLOCK, counts.shape[1])
    factor_rows = fact_half.T.reshape(rows_total // BLOCK, BLOCK, fact_half.shape[0])

    def block_error(pair):
        block_counts, block_factors = pair
        recon = jnp.dot(block_factors, load_half, preferred_element_type=jnp.float32)
        return jnp.mean(jnp.square(block_counts.astype(jnp.float32) - recon), axis=1)

    fit_error = lax.map(block_error, (count_blocks, factor_rows)).reshape(-1)
    return factors, loadings, fit_error
```

```python
import functools

import jax
import jax.numpy as jnp
from jax import lax
from jax.experimental import pallas as pl
from jax.experimental.pallas import tpu as pltpu
from jax.sharding import PartitionSpec as P

ITERS = 2


graph_weight = 0.5
epsilon = 1e-09
MESH = pl.DeviceIdType.MESH
f32 = jnp.float32
bf16 = jnp.bfloat16
ORDER = (2, 1, 3, 0)
LANES = 128


def lanes_of(shape):
    return lax.broadcasted_iota(jnp.int32, shape, len(shape) - 1)


def roll(x, shift):
    shift %= x.shape[-1]
    return pltpu.roll(x, shift, x.ndim - 1) if shift else x


def pack_chunk(v):
    tiles = [v[:, LANES * t : LANES * (t + 1)] for t in range(5)]
    lane = lanes_of((64, LANES))
    small = lanes_of((16, LANES))
    pieces = []
    for p in range(4):
        first = tiles[p] if p == 0 else roll(jnp.where(lane >= 32 * p, tiles[p], tiles[p + 1]), -32 * p)
        pieces.append(jnp.concatenate([first, pack_rest(tiles[p + 1], 32 * p, small)], axis=0))
    return pieces


def pack_rest(tile, at, small):
    rest = roll(tile[0:16], -at)
    for j in range(1, 4):
        rest = jnp.where(small >= 32 * j, roll(tile[16 * j : 16 * j + 16], 32 * j - at), rest)
    return rest


def unpack_chunk(pieces):
    lane = lanes_of((64, LANES))
    firsts = [roll(x[0:64], 32 * p) for p, x in enumerate(pieces)]
    rests = [
        jnp.concatenate([roll(x[64:80], 32 * p - 32 * j) for j in range(4)], axis=0)
        for p, x in enumerate(pieces)
    ]
    tiles = []
    for t in range(5):
        tile = None
        if t >= 1:
            tile = jnp.where(lane >= 32 * (t - 1), rests[t - 1], firsts[t - 1])
        if t < 4:
            tile = firsts[0] if t == 0 else jnp.where(lane >= 32 * t, firsts[t], tile)
        tiles.append(tile)
    return tiles


def unpack_piece(x):
    rest = jnp.concatenate([roll(x[64:80], -32 * j) for j in range(4)], axis=0)
    rest = jnp.where(lanes_of((64, LANES)) < 32, rest, 0.0)
    return jnp.concatenate([x[0:64], rest], axis=1)


def pack_piece(v):
    return jnp.concatenate(
        [v[:, 0:LANES], pack_rest(v[:, LANES : 2 * LANES], 0, lanes_of((16, LANES)))], axis=0
    )


def halves(x):
    hi = x.astype(bf16)
    return hi, (x - hi.astype(f32)).astype(bf16)


def dot_t(a, b):
    return lax.dot_general(a, b, (((1,), (1,)), ((), ())), preferred_element_type=f32)


def dot(a, b):
    return jnp.dot(a, b, preferred_element_type=f32)


def packed_gram(x):
    full = dot_t(x, x)
    q = full[0:64] + full[64:128]
    q = q + roll(q, 64)
    return jnp.where(lanes_of((32, LANES)) < 64, q[0:32], q[32:64])


def gram_operand(s):
    turned = roll(s, 64)
    low = lanes_of((32, LANES)) < 64
    twice = jnp.concatenate([jnp.where(low, s, turned), jnp.where(low, turned, s)], axis=0)
    hi, lo = halves(twice)
    return jnp.concatenate([hi, lo], axis=1)


def kernel(
    n, offs, counts, cell_init, load_init, weights, factors_out, load_out, fit_out,
    cbuf, wbuf, fcur, xf, fb0, fb1, lcur, lhf, dt, gt, deg, csq,
    fg_own, fg_got, fg_sum, fg_sib, lg_own, lg_got, lg_sum, lg_sib,
    a_buf, a_got, b_buf, b_got, c_buf, c_got, lh_all,
    csem, wsem, halo_s, halo_r, g_s, g_r, gs_s, gs_r,
    a_s, a_r, b_s, b_r, c_s, c_r, l_s, l_r, ls_s, ls_r,
):
    me = lax.axis_index("cell")
    core = lax.rem(me, 2)
    y = lax.rem(lax.div(me, 2), 2)
    z = lax.div(me, 4)
    sib = me + 1 - 2 * core
    ynb = me + 2 - 4 * y
    line = lax.div(me, 2)
    nline = n // 2
    nb = weights.shape[0]
    fbs = (fb0, fb1)

    barrier = pltpu.get_barrier_semaphore()
    for j in range(1, n):
        pl.semaphore_signal(barrier, inc=1, device_id={"cell": lax.rem(me + j, n)}, device_id_type=MESH)

    width = 640
    chunk_at = [pl.multiple_of(lax.rem(z + o, n // 4) * width, width) for o in ORDER]
    ccopies = []
    for i in range(4):
        cp = pltpu.make_async_copy(
            counts.at[:, pl.ds(chunk_at[i], width)], cbuf.at[:, pl.ds(chunk_at[i], width)], csem.at[i]
        )
        cp.start()
        ccopies.append(cp)
    wcopy = pltpu.make_async_copy(weights, wbuf, wsem)
    wcopy.start()

    lcur[...] = jnp.zeros_like(lcur)
    lcur[:, 0:160] = load_init[...]
    sends = []

    def push(src, dst, ssem, rsem, dev):
        cp = pltpu.make_async_remote_copy(
            src_ref=src, dst_ref=dst, send_sem=ssem, recv_sem=rsem, device_id={"cell": dev}, device_id_type=MESH
        )
        cp.start()
        sends.append(cp)
        return cp

    def set_factors(it, b, value):
        at = pl.multiple_of(b * LANES, LANES)
        hi, lo = halves(value)
        xf[0:64, pl.ds(at, LANES)] = hi
        xf[64:128, pl.ds(at, LANES)] = lo
        if it < ITERS:
            fbs[it][b + 2] = hi

    def first_factors(b, carry):
        set_factors(0, b, cell_init[:, pl.ds(pl.multiple_of(b * LANES, LANES), LANES)])
        return carry

    lax.fori_loop(0, nb, first_factors, 0)
    pl.semaphore_wait(barrier, n - 1)

    def halo(it, go):
        fb = fbs[it]
        left = pltpu.make_async_remote_copy(
            src_ref=fb.at[pl.ds(2, 2)], dst_ref=fb.at[pl.ds(nb + 2, 2)], send_sem=halo_s.at[it, 0],
            recv_sem=halo_r.at[it, 0], device_id={"cell": lax.rem(me + n - 1, n)}, device_id_type=MESH,
        )
        right = pltpu.make_async_remote_copy(
            src_ref=fb.at[pl.ds(nb, 2)], dst_ref=fb.at[pl.ds(0, 2)], send_sem=halo_s.at[it, 1],
            recv_sem=halo_r.at[it, 1], device_id={"cell": lax.rem(me + 1, n)}, device_id_type=MESH,
        )
        if go == "start":
            @pl.when(me > 0)
            def _():
                left.start()

            @pl.when(me < n - 1)
            def _():
                right.start()

            @pl.when(me == 0)
            def _():
                fb[0:2] = jnp.zeros((2, 64, LANES), bf16)

            @pl.when(me == n - 1)
            def _():
                fb[nb + 2 : nb + 4] = jnp.zeros((2, 64, LANES), bf16)
        elif go == "recv":
            @pl.when(me < n - 1)
            def _():
                left.wait_recv()

            @pl.when(me > 0)
            def _():
                right.wait_recv()
        else:
            @pl.when(me > 0)
            def _():
                left.wait_send()

            @pl.when(me < n - 1)
            def _():
                right.wait_send()

    def gram_start(k, it, own, got, x):
        own[it] = packed_gram(x)
        return [
            push(own.at[it], got.at[it, j - 1], g_s.at[k, it, j - 1], g_r.at[k, it, j - 1],
                 2 * lax.rem(line + j, nline) + core)
            for j in range(1, nline)
        ]

    def gram_middle(k, it, copies, own, got, total, far):
        acc = own[it]
        for j, cp in enumerate(copies):
            cp.wait_recv()
            acc = acc + got[it, j]
        total[it] = acc
        return push(total.at[it], far.at[it], gs_s.at[k, it], gs_r.at[k, it], sib)

    def gram_end(it, copy, total, far):
        copy.wait_recv()
        return gram_operand(total[it] + far[it])

    def graph(it, start, stop):
        fb = fbs[it]

        def step(b, carry):
            acc = jnp.zeros((80, LANES), f32)
            for s in range(3):
                picked = fb[b + 2 + offs[b, s]]
                lhs = jnp.concatenate([picked, jnp.ones((16, LANES), bf16)], axis=0)
                acc = acc + dot_t(lhs, wbuf[b, s])
            gt[b] = graph_weight * acc[0:64]
            if it == 0:
                deg[b] = graph_weight * acc[64:72]
            return carry

        lax.fori_loop(start, stop, step, 0, unroll=2)

    def squares(start, stop):
        def step(b, carry):
            rows = pl.ds(pl.multiple_of(b * LANES, LANES), LANES)
            acc = jnp.zeros((LANES, LANES), f32)
            for t in range(cbuf.shape[1] // LANES):
                c = cbuf[rows, LANES * t : LANES * (t + 1)].astype(f32)
                acc = acc + c * c
            hi, lo = halves(acc)
            ones = jnp.ones((16, LANES), bf16)
            csq[b] = (dot_t(ones, hi) + dot_t(ones, lo))[0:8]
            return carry

        lax.fori_loop(start, stop, step, 0)

    for it in range(ITERS):
        last = it == ITERS - 1
        halo(it, "start")
        fgc = gram_start(0, it, fg_own, fg_got, xf[...])

        acopies, bcopies, ccs = [], [], []

        def reduce_core(i):
            acopies[i].wait_recv()
            b_buf[it, i] = a_buf[it, i, core] + a_got[it, i]
            bcopies.append(push(b_buf.at[it, i, 1 - y], b_got.at[it, i], b_s.at[it, i], b_r.at[it, i], ynb))

        def reduce_y(i):
            bcopies[i].wait_recv()
            c_buf[it, i] = b_buf[it, i, y] + b_got[it, i]
            if i < 3:
                dev = 4 * lax.rem(z + ORDER[i], 4) + 2 * y + core
                ccs.append(push(c_buf.at[it, i], c_got.at[it, i], c_s.at[it, i], c_r.at[it, i], dev))

        fgm = None
        for i in range(4):
            if it == 0:
                ccopies[i].wait()
            v = dot(xf[0:64, :], cbuf[:, pl.ds(chunk_at[i], width)])
            for p, piece in enumerate(pack_chunk(v)):
                a_buf[it, i, p % 2, p // 2] = piece
            acopies.append(
                push(a_buf.at[it, i, 1 - core], a_got.at[it, i], a_s.at[it, i], a_r.at[it, i], sib)
            )
            if i >= 1:
                reduce_core(i - 1)
            if i >= 2:
                reduce_y(i - 2)
            if i == 2:
                fgm = gram_middle(0, it, fgc, fg_own, fg_got, fg_sum, fg_sib)
        if it == 0:
            wcopy.wait()
        halo(it, "recv")
        graph(it, 0, nb // 4)
        reduce_core(3)
        reduce_y(2)
        graph(it, nb // 4, nb // 2)
        reduce_y(3)
        fg = gram_end(it, fgm, fg_sum, fg_sib)
        own = lcur[...]
        lhi, llo = halves(own)
        under = dot(fg, jnp.concatenate([lhi, llo, lhi, llo], axis=0)) + epsilon
        sums = c_buf[it, 3]
        for i in range(3):
            ccs[i].wait_recv()
            sums = sums + c_got[it, i]
        own = own * unpack_piece(sums) / under
        lcur[...] = own
        lh_all[it, me] = pack_piece(own).astype(bf16)
        lcs = [
            push(lh_all.at[it, me], lh_all.at[it, me], l_s.at[it, j - 1], l_r.at[it, j - 1],
                 2 * lax.rem(line + j, nline) + core)
            for j in range(1, nline)
        ]
        sibs = [push(lh_all.at[it, me], lh_all.at[it, me], ls_s.at[it, 0], ls_r.at[it, 0], sib)]
        lhi, llo = halves(own)
        lgc = gram_start(1, it, lg_own, lg_got, jnp.concatenate([lhi, llo], axis=0))
        if last:
            load_out[...] = own[:, 0:160]
        graph(it, nb // 2, nb)
        for j in range(1, nline):
            at = 2 * lax.rem(line + nline - j, nline) + core
            pltpu.make_async_remote_copy(
                src_ref=lh_all.at[it, at], dst_ref=lh_all.at[it, at], send_sem=l_s.at[it, j - 1],
                recv_sem=l_r.at[it, j - 1], device_id={"cell": at}, device_id_type=MESH,
            ).wait_recv()
            sibs.append(push(lh_all.at[it, at], lh_all.at[it, at], ls_s.at[it, j], ls_r.at[it, j], sib))
        if last:
            squares(0, nb)
        for cp in sibs:
            cp.wait_recv()
        for c in range(n // 4):
            pieces = [lh_all[it, 4 * c + p].astype(f32) for p in range(4)]
            for t, tile in enumerate(unpack_chunk(pieces)):
                at = width * c + LANES * t
                lhf[:, at : at + LANES] = tile.astype(bf16)

        def data(i, carry):
            rows = pl.ds(pl.multiple_of(i * 256, 256), 256)
            part = dot_t(lhf[...], cbuf[rows, :])
            dt[2 * i] = part[:, 0:LANES]
            dt[2 * i + 1] = part[:, LANES:]
            return carry

        lax.fori_loop(0, nb // 4, data, 0)
        lgm = gram_middle(1, it, lgc, lg_own, lg_got, lg_sum, lg_sib)
        lax.fori_loop(nb // 4, nb // 2, data, 0)
        lg = gram_end(it, lgm, lg_sum, lg_sib)
        if last:
            twice = dot_t(lhf[...], jnp.concatenate([lhf[...], lhf[...]], axis=0))
            mhi, mlo = halves(twice)
            pair = jnp.where(lanes_of((64, LANES)) < 64, mhi.astype(f32), mlo.astype(f32)).astype(bf16)

        source = cell_init if it == 0 else fcur
        target = factors_out if last else fcur

        def update(b, carry):
            cols = pl.ds(pl.multiple_of(b * LANES, LANES), LANES)
            f = source[:, cols]
            x = xf[:, cols]
            under = dot(lg, jnp.concatenate([x, x], axis=0)) + deg[b][0:1] * f + epsilon
            new = f * (dt[b] + gt[b]) / under
            target[:, cols] = new
            if last:
                hi = new.astype(bf16)
                recon2 = dot(pair, jnp.concatenate([hi, hi], axis=0))
                inner = jnp.sum(hi.astype(f32) * (recon2 - 2.0 * dt[b]), axis=0, keepdims=True)
                fit_out[pl.ds(b, 1), :] = (csq[b][0:1] + inner) * (1.0 / cbuf.shape[1])
            else:
                set_factors(it + 1, b, new)
            return carry

        lax.fori_loop(0, nb, update, 0, unroll=2)

    for cp in sends:
        cp.wait_send()
    for it in range(ITERS):
        halo(it, "send")


def fused(n, counts, cell_init, load_init, band_offsets, band_weights):
    cells, genes = counts.shape
    nb = band_weights.shape[0]
    T = ITERS
    V = pltpu.VMEM
    D = pltpu.SemaphoreType.DMA
    scratch = [
        V((cells, genes), bf16), V(band_weights.shape, bf16), V((64, cells), f32), V((128, cells), bf16),
        V((nb + 4, 64, 128), bf16), V((nb + 4, 64, 128), bf16), V((64, 256), f32), V((64, genes), bf16),
        V((nb, 64, 128), f32), V((nb, 64, 128), f32), V((nb, 8, 128), f32), V((nb, 8, 128), f32),
    ]
    for _ in range(2):
        scratch += [V((T, 32, 128), f32), V((T, n // 2 - 1, 32, 128), f32), V((T, 32, 128), f32), V((T, 32, 128), f32)]
    scratch += [
        V((T, 4, 2, 2, 80, 128), f32), V((T, 4, 2, 80, 128), f32),
        V((T, 4, 2, 80, 128), f32), V((T, 4, 80, 128), f32),
        V((T, 4, 80, 128), f32), V((T, 3, 80, 128), f32),
        V((T, n, 80, 128), bf16),
        D((4,)), D(()), D((T, 2)), D((T, 2)),
        D((2, T, n // 2 - 1)), D((2, T, n // 2 - 1)), D((2, T)), D((2, T)),
        D((T, 4)), D((T, 4)), D((T, 4)), D((T, 4)), D((T, 3)), D((T, 3)),
        D((T, n // 2 - 1)), D((T, n // 2 - 1)), D((T, n // 2)), D((T, n // 2)),
    ]
    vm = pl.BlockSpec(memory_space=pltpu.VMEM)
    hbm = pl.BlockSpec(memory_space=pl.ANY)
    factors, loadings, fit = pl.pallas_call(
        functools.partial(kernel, n),
        out_shape=(
            jax.ShapeDtypeStruct(cell_init.shape, f32),
            jax.ShapeDtypeStruct(load_init.shape, f32),
            jax.ShapeDtypeStruct((nb, 128), f32),
        ),
        in_specs=[pl.BlockSpec(memory_space=pltpu.SMEM), hbm, vm, vm, hbm],
        out_specs=(vm, vm, vm),
        scratch_shapes=scratch,
        compiler_params=pltpu.CompilerParams(
            collective_id=0, has_side_effects=True, vmem_limit_bytes=48 * 1024 * 1024
        ),
    )(band_offsets, counts, cell_init, load_init, band_weights)
    return factors, loadings, fit.reshape(-1)


def extended(cells, sides, width):
    for axis, dim in sides:
        count = lax.axis_size(axis)
        ends = count - 1
        head = lax.slice_in_dim(cells, 0, width, axis=dim)
        tail = lax.slice_in_dim(cells, cells.shape[dim] - width, cells.shape[dim], axis=dim)
        cells = jnp.concatenate(
            [
                lax.ppermute(tail, axis, [(i, (i + 1) % count) for i in range(ends)]),
                cells,
                lax.ppermute(head, axis, [((i + 1) % count, i) for i in range(ends)]),
            ],
            axis=dim,
        )
    return cells


def make_gene_rows(counts, fact_half):
    return lax.dot_general(
        counts, fact_half, (((0,), (1,)), ((), ())), preferred_element_type=jnp.float32
    )


def body(counts, cell_init, load_init, band_offsets, band_weights):
    count = lax.axis_size("cell")
    if count == 16 and load_init.shape == (64, 160) and counts.shape[0] == 128 * band_weights.shape[0]:
        return fused(count, counts, cell_init, load_init, band_offsets, band_weights)
    highest = lax.Precision.HIGHEST
    factors = cell_init
    loadings = load_init
    rank = factors.shape[0]
    nblocks = band_weights.shape[0]
    block = band_weights.shape[-1]
    degree = jnp.sum(band_weights.astype(jnp.float32), axis=(1, 3)).reshape(-1)
    positions = jnp.arange(nblocks, dtype=jnp.int32)[:, None] + 2 + band_offsets
    load_half = loadings.astype(jnp.bfloat16)
    for sweep in range(ITERS):
        fact_half = factors.astype(jnp.bfloat16)
        local_gram = jnp.dot(factors, factors.T, precision=highest)
        own_sums = lax.psum_scatter(
            make_gene_rows(counts, fact_half), "cell", scatter_dimension=0, tiled=True
        )
        factor_gram = lax.psum(local_gram, "cell")
        loadings = (
            loadings * own_sums.T / (jnp.dot(factor_gram, loadings, precision=highest) + epsilon)
        )
        load_gram = lax.psum(jnp.dot(loadings, loadings.T, precision=highest), "cell")
        load_half = lax.all_gather(loadings.astype(jnp.bfloat16), "cell", axis=1, tiled=True)
        data_term = lax.dot_general(
            load_half, counts, (((1,), (1,)), ((), ())), preferred_element_type=jnp.float32
        )
        padded = extended(fact_half, (("cell", 1),), 2 * block)
        blocks = padded.reshape(rank, nblocks + 4, block)
        picked = jnp.take(blocks, positions, axis=1)
        result = jnp.einsum(
            "nsij,knsj->kni", band_weights, picked, preferred_element_type=jnp.float32
        )
        graph_term = result.reshape(rank, nblocks * block)
        numer = data_term + graph_weight * graph_term
        denom = (
            jnp.dot(load_gram, factors, precision=highest)
            + graph_weight * degree[None, :] * factors
            + epsilon
        )
        factors = factors * numer / denom
    fact_half = factors.astype(jnp.bfloat16)
    recon = lax.dot_general(
        fact_half, load_half, (((0,), (0,)), ((), ())), preferred_element_type=jnp.float32
    )
    fit_error = jnp.mean(jnp.square(counts.astype(jnp.float32) - recon), axis=1)
    return (factors, loadings, fit_error)


def solution(mesh):
    in_specs = (
        P(("grp", "cell"), None),
        P(None, ("grp", "cell")),
        P(None, ("grp", "cell")),
        P(("grp", "cell"), None),
        P(("grp", "cell"), None, None, None),
    )
    out_specs = (P(None, ("grp", "cell")), P(None, ("grp", "cell")), P(("grp", "cell")))
    return jax.shard_map(body, mesh=mesh, in_specs=in_specs, out_specs=out_specs, check_vma=False)
```

```python
import functools

import jax
import jax.numpy as jnp
from jax import lax
from jax.experimental import pallas as pl
from jax.experimental.pallas import tpu as pltpu
from jax.sharding import PartitionSpec as P

ITERS = 2


graph_weight = 0.5
epsilon = 1e-09
MESH = pl.DeviceIdType.MESH
f32 = jnp.float32
bf16 = jnp.bfloat16
ORDER = (2, 1, 3, 0)
LANES = 128


def lanes_of(shape):
    return lax.broadcasted_iota(jnp.int32, shape, len(shape) - 1)


def roll(x, shift):
    shift %= x.shape[-1]
    return pltpu.roll(x, shift, x.ndim - 1) if shift else x


def pack_chunk(v):
    tiles = [v[:, LANES * t : LANES * (t + 1)] for t in range(5)]
    lane = lanes_of((64, LANES))
    small = lanes_of((16, LANES))
    pieces = []
    for p in range(4):
        first = tiles[p] if p == 0 else roll(jnp.where(lane >= 32 * p, tiles[p], tiles[p + 1]), -32 * p)
        pieces.append(jnp.concatenate([first, pack_rest(tiles[p + 1], 32 * p, small)], axis=0))
    return pieces


def pack_rest(tile, at, small):
    rest = roll(tile[0:16], -at)
    for j in range(1, 4):
        rest = jnp.where(small >= 32 * j, roll(tile[16 * j : 16 * j + 16], 32 * j - at), rest)
    return rest


def unpack_chunk(pieces):
    lane = lanes_of((64, LANES))
    firsts = [roll(x[0:64], 32 * p) for p, x in enumerate(pieces)]
    rests = [
        jnp.concatenate([roll(x[64:80], 32 * p - 32 * j) for j in range(4)], axis=0)
        for p, x in enumerate(pieces)
    ]
    tiles = []
    for t in range(5):
        tile = None
        if t >= 1:
            tile = jnp.where(lane >= 32 * (t - 1), rests[t - 1], firsts[t - 1])
        if t < 4:
            tile = firsts[0] if t == 0 else jnp.where(lane >= 32 * t, firsts[t], tile)
        tiles.append(tile)
    return tiles


def unpack_piece(x):
    rest = jnp.concatenate([roll(x[64:80], -32 * j) for j in range(4)], axis=0)
    rest = jnp.where(lanes_of((64, LANES)) < 32, rest, 0.0)
    return jnp.concatenate([x[0:64], rest], axis=1)


def pack_piece(v):
    return jnp.concatenate(
        [v[:, 0:LANES], pack_rest(v[:, LANES : 2 * LANES], 0, lanes_of((16, LANES)))], axis=0
    )


def halves(x):
    hi = x.astype(bf16)
    return hi, (x - hi.astype(f32)).astype(bf16)


def dot_t(a, b):
    return lax.dot_general(a, b, (((1,), (1,)), ((), ())), preferred_element_type=f32)


def dot(a, b):
    return jnp.dot(a, b, preferred_element_type=f32)


def packed_gram(x):
    full = dot_t(x, x)
    q = full[0:64] + full[64:128]
    q = q + roll(q, 64)
    return jnp.where(lanes_of((32, LANES)) < 64, q[0:32], q[32:64])


def gram_operand(s):
    turned = roll(s, 64)
    low = lanes_of((32, LANES)) < 64
    twice = jnp.concatenate([jnp.where(low, s, turned), jnp.where(low, turned, s)], axis=0)
    hi, lo = halves(twice)
    return jnp.concatenate([hi, lo], axis=1)


def kernel(
    n, offs_in, counts, cell_in, load_in, weights, factors_out, load_out, fit_out,
    offs, cell_init, load_init, cbuf, wbuf, fcur, xf, fb0, fb1, lcur, lhf, dt, gt, deg, csq,
    fg_own, fg_got, lg_own, lg_got,
    a_buf, a_got, b_buf, b_got, c_buf, c_got, lh_all,
    isem, csem, wsem, halo_s, halo_r, g_s, g_r,
    a_s, a_r, b_s, b_r, c_s, c_r, l_s, l_r, ls_s, ls_r,
):
    me = lax.axis_index("cell")
    core = lax.rem(me, 2)
    y = lax.rem(lax.div(me, 2), 2)
    z = lax.div(me, 4)
    sib = me + 1 - 2 * core
    ynb = me + 2 - 4 * y
    nb = weights.shape[0]
    fbs = (fb0, fb1)

    barrier = pltpu.get_barrier_semaphore()
    for j in range(1, n):
        pl.semaphore_signal(barrier, inc=1, device_id={"cell": lax.rem(me + j, n)}, device_id_type=MESH)

    icopies = [
        pltpu.make_async_copy(src, dst, isem.at[i])
        for i, (src, dst) in enumerate(((cell_in, cell_init), (load_in, load_init), (offs_in, offs)))
    ]
    for cp in icopies:
        cp.start()
    width = 640
    chunk_at = [pl.multiple_of(lax.rem(z + o, n // 4) * width, width) for o in ORDER]
    ccopies = []
    for i in range(4):
        cp = pltpu.make_async_copy(
            counts.at[:, pl.ds(chunk_at[i], width)], cbuf.at[:, pl.ds(chunk_at[i], width)], csem.at[i]
        )
        cp.start()
        ccopies.append(cp)
    wcopy = pltpu.make_async_copy(weights, wbuf, wsem)
    wcopy.start()

    for cp in icopies:
        cp.wait()
    lcur[...] = jnp.zeros_like(lcur)
    lcur[:, 0:160] = load_init[...]
    sends = []

    def push(src, dst, ssem, rsem, dev):
        cp = pltpu.make_async_remote_copy(
            src_ref=src, dst_ref=dst, send_sem=ssem, recv_sem=rsem, device_id={"cell": dev}, device_id_type=MESH
        )
        cp.start()
        sends.append(cp)
        return cp

    def set_factors(it, b, value):
        at = pl.multiple_of(b * LANES, LANES)
        hi, lo = halves(value)
        xf[0:64, pl.ds(at, LANES)] = hi
        xf[64:128, pl.ds(at, LANES)] = lo
        if it < ITERS:
            fbs[it][b + 2] = hi

    def first_factors(b, carry):
        set_factors(0, b, cell_init[:, pl.ds(pl.multiple_of(b * LANES, LANES), LANES)])
        return carry

    lax.fori_loop(0, nb, first_factors, 0)
    pl.semaphore_wait(barrier, n - 1)

    def halo(it, go):
        fb = fbs[it]
        left = pltpu.make_async_remote_copy(
            src_ref=fb.at[pl.ds(2, 2)], dst_ref=fb.at[pl.ds(nb + 2, 2)], send_sem=halo_s.at[it, 0],
            recv_sem=halo_r.at[it, 0], device_id={"cell": lax.rem(me + n - 1, n)}, device_id_type=MESH,
        )
        right = pltpu.make_async_remote_copy(
            src_ref=fb.at[pl.ds(nb, 2)], dst_ref=fb.at[pl.ds(0, 2)], send_sem=halo_s.at[it, 1],
            recv_sem=halo_r.at[it, 1], device_id={"cell": lax.rem(me + 1, n)}, device_id_type=MESH,
        )
        if go == "start":
            @pl.when(me > 0)
            def _():
                left.start()

            @pl.when(me < n - 1)
            def _():
                right.start()

            @pl.when(me == 0)
            def _():
                fb[0:2] = jnp.zeros((2, 64, LANES), bf16)

            @pl.when(me == n - 1)
            def _():
                fb[nb + 2 : nb + 4] = jnp.zeros((2, 64, LANES), bf16)
        elif go == "recv":
            @pl.when(me < n - 1)
            def _():
                left.wait_recv()

            @pl.when(me > 0)
            def _():
                right.wait_recv()
        else:
            @pl.when(me > 0)
            def _():
                left.wait_send()

            @pl.when(me < n - 1)
            def _():
                right.wait_send()

    def gram_send(k, it, own, got, step, x):
        own[it, step] = x
        if step < 2:
            devs = [(sib, ynb)[step]]
        else:
            devs = [4 * lax.rem(z + o, 4) + 2 * y + core for o in (2, 1, 3)]
        return [
            push(own.at[it, step], got.at[it, step + j], g_s.at[k, it, step + j], g_r.at[k, it, step + j], dev)
            for j, dev in enumerate(devs)
        ]

    def gram_next(k, it, copies, own, got, step):
        copies[0].wait_recv()
        return gram_send(k, it, own, got, step, own[it, step - 1] + got[it, step - 1])

    def gram_end(it, copies, own, got):
        acc = own[it, 2]
        for j, cp in enumerate(copies):
            cp.wait_recv()
            acc = acc + got[it, 2 + j]
        return gram_operand(acc)

    def graph(it, start, stop):
        fb = fbs[it]

        def step(b, carry):
            acc = jnp.zeros((80, LANES), f32)
            for s in range(3):
                picked = fb[b + 2 + offs[b, s]]
                lhs = jnp.concatenate([picked, jnp.ones((16, LANES), bf16)], axis=0)
                acc = acc + dot_t(lhs, wbuf[b, s])
            gt[b] = graph_weight * acc[0:64]
            if it == 0:
                deg[b] = graph_weight * acc[64:72]
            return carry

        lax.fori_loop(start, stop, step, 0, unroll=2)

    def squares(start, stop):
        def step(b, carry):
            rows = pl.ds(pl.multiple_of(b * LANES, LANES), LANES)
            acc = jnp.zeros((LANES, LANES), f32)
            for t in range(cbuf.shape[1] // LANES):
                c = cbuf[rows, LANES * t : LANES * (t + 1)].astype(f32)
                acc = acc + c * c
            hi, lo = halves(acc)
            ones = jnp.ones((16, LANES), bf16)
            csq[b] = (dot_t(ones, hi) + dot_t(ones, lo))[0:8]
            return carry

        lax.fori_loop(start, stop, step, 0)

    for it in range(ITERS):
        last = it == ITERS - 1
        halo(it, "start")
        fgc = gram_send(0, it, fg_own, fg_got, 0, packed_gram(xf[...]))

        acopies, bcopies, ccs = [], [], []

        def reduce_core(i):
            acopies[i].wait_recv()
            b_buf[it, i] = a_buf[it, i, core] + a_got[it, i]
            bcopies.append(push(b_buf.at[it, i, 1 - y], b_got.at[it, i], b_s.at[it, i], b_r.at[it, i], ynb))

        def reduce_y(i):
            bcopies[i].wait_recv()
            c_buf[it, i] = b_buf[it, i, y] + b_got[it, i]
            if i < 3:
                dev = 4 * lax.rem(z + ORDER[i], 4) + 2 * y + core
                ccs.append(push(c_buf.at[it, i], c_got.at[it, i], c_s.at[it, i], c_r.at[it, i], dev))

        for i in range(4):
            if it == 0:
                ccopies[i].wait()
            v = dot(xf[0:64, :], cbuf[:, pl.ds(chunk_at[i], width)])
            for p, piece in enumerate(pack_chunk(v)):
                a_buf[it, i, p % 2, p // 2] = piece
            acopies.append(
                push(a_buf.at[it, i, 1 - core], a_got.at[it, i], a_s.at[it, i], a_r.at[it, i], sib)
            )
            if i >= 1:
                reduce_core(i - 1)
            if i >= 2:
                reduce_y(i - 2)
            if i == 0 or i == 2:
                fgc = gram_next(0, it, fgc, fg_own, fg_got, 1 + i // 2)
        if it == 0:
            wcopy.wait()
        halo(it, "recv")
        graph(it, 0, nb // 4)
        reduce_core(3)
        reduce_y(2)
        graph(it, nb // 4, nb // 2)
        reduce_y(3)
        graph(it, nb // 2, nb)
        squares(it * nb // 2, it * nb // 2 + nb // 4)
        fg = gram_end(it, fgc, fg_own, fg_got)
        own = lcur[...]
        lhi, llo = halves(own)
        under = dot(fg, jnp.concatenate([lhi, llo, lhi, llo], axis=0)) + epsilon
        sums = c_buf[it, 3]
        for i in range(3):
            ccs[i].wait_recv()
            sums = sums + c_got[it, i]
        own = own * unpack_piece(sums) / under
        lcur[...] = own
        lh_all[it, me] = pack_piece(own).astype(bf16)
        def piece_of(o, t):
            return 4 * lax.rem(z + 4 - o, 4) + 2 * (y if t == 0 else 1 - y) + core

        def spread(o, t):
            dev = 4 * lax.rem(z + o, 4) + 2 * (y if t == 0 else 1 - y) + core
            m = 2 * o + t
            lcs[m] = push(lh_all.at[it, me], lh_all.at[it, me], l_s.at[it, m - 1], l_r.at[it, m - 1], dev)

        def hand_on(o, t):
            m, at = 2 * o + t, piece_of(o, t)
            if m:
                pltpu.make_async_remote_copy(
                    src_ref=lh_all.at[it, at], dst_ref=lh_all.at[it, at], send_sem=l_s.at[it, m - 1],
                    recv_sem=l_r.at[it, m - 1], device_id={"cell": at}, device_id_type=MESH,
                ).wait_recv()
            sibs[m] = push(lh_all.at[it, at], lh_all.at[it, at], ls_s.at[it, m], ls_r.at[it, m], sib)

        lcs, sibs = {}, {}
        spread(0, 1)
        hand_on(0, 0)
        for o, t in ((1, 0), (3, 0), (1, 1), (3, 1), (2, 0), (2, 1)):
            spread(o, t)
        lhi, llo = halves(own)
        lgc = gram_send(1, it, lg_own, lg_got, 0, packed_gram(jnp.concatenate([lhi, llo], axis=0)))
        if last:
            load_out[...] = own[:, 0:160]

        def data(o):
            for t in range(2):
                sibs[2 * o + t].wait_recv()
            c = lax.rem(z + 4 - o, 4)
            pieces = [lh_all[it, 4 * c + p].astype(f32) for p in range(4)]
            cols = pl.ds(pl.multiple_of(c * width, width), width)
            lhf[:, cols] = jnp.concatenate(unpack_chunk(pieces), axis=1).astype(bf16)
            tall = 512

            def step(i, carry):
                rows = pl.ds(pl.multiple_of(i * tall, tall), tall)
                part = dot_t(cbuf[rows, cols], lhf[:, cols])
                dt[rows, :] = part if o == 0 else dt[rows, :] + part
                return carry

            lax.fori_loop(0, nb * LANES // tall, step, 0)

        squares(it * nb // 2 + nb // 4, (it + 1) * nb // 2)
        hand_on(0, 1)
        lgc = gram_next(1, it, lgc, lg_own, lg_got, 1)
        hand_on(1, 0)
        hand_on(1, 1)
        data(0)
        hand_on(3, 0)
        hand_on(3, 1)
        lgc = gram_next(1, it, lgc, lg_own, lg_got, 2)
        data(1)
        hand_on(2, 0)
        hand_on(2, 1)
        data(3)
        data(2)
        lg = gram_end(it, lgc, lg_own, lg_got)
        if last:
            twice = dot_t(lhf[...], jnp.concatenate([lhf[...], lhf[...]], axis=0))
            mhi, mlo = halves(twice)
            pair = jnp.where(lanes_of((64, LANES)) < 64, mhi.astype(f32), mlo.astype(f32)).astype(bf16)

        source = cell_init if it == 0 else fcur
        target = factors_out if last else fcur

        def update(pair_at, carry):
            cols = pl.ds(pl.multiple_of(pair_at * 2 * LANES, 2 * LANES), 2 * LANES)
            x = xf[:, cols]
            product = dot(lg, jnp.concatenate([x, x], axis=0))
            news, datas = [], []
            for h in range(2):
                b = 2 * pair_at + h
                at = pl.ds(pl.multiple_of(b * LANES, LANES), LANES)
                f = source[:, at]
                data_term = dt[at, :].T
                under = product[:, h * LANES : (h + 1) * LANES] + deg[b][0:1] * f + epsilon
                new = f * (data_term + gt[b]) / under
                target[:, at] = new
                news.append(new)
                datas.append(data_term)
                if not last:
                    set_factors(it + 1, b, new)
            if last:
                hi = jnp.concatenate(news, axis=1).astype(bf16)
                recon2 = dot(pair, jnp.concatenate([hi, hi], axis=0)) - 2.0 * jnp.concatenate(datas, axis=1)
                inner = jnp.sum(hi.astype(f32) * recon2, axis=0, keepdims=True)
                for h in range(2):
                    b = 2 * pair_at + h
                    total = csq[b][0:1] + inner[:, h * LANES : (h + 1) * LANES]
                    fit_out[pl.ds(b, 1), :] = total * (1.0 / cbuf.shape[1])
            return carry

        lax.fori_loop(0, nb // 2, update, 0, unroll=2)

    for cp in sends:
        cp.wait_send()
    for it in range(ITERS):
        halo(it, "send")


def fused(n, counts, cell_init, load_init, band_offsets, band_weights):
    cells, genes = counts.shape
    nb = band_weights.shape[0]
    T = ITERS
    V = pltpu.VMEM
    D = pltpu.SemaphoreType.DMA
    scratch = [
        pltpu.SMEM(band_offsets.shape, jnp.int32), V((64, cells), f32), V((64, 160), f32),
        V((cells, genes), bf16), V(band_weights.shape, bf16), V((64, cells), f32), V((128, cells), bf16),
        V((nb + 4, 64, 128), bf16), V((nb + 4, 64, 128), bf16), V((64, 256), f32), V((64, genes), bf16),
        V((cells, 64), f32), V((nb, 64, 128), f32), V((nb, 8, 128), f32), V((nb, 8, 128), f32),
    ]
    for _ in range(2):
        scratch += [V((T, 3, 32, 128), f32), V((T, 5, 32, 128), f32)]
    scratch += [
        V((T, 4, 2, 2, 80, 128), f32), V((T, 4, 2, 80, 128), f32),
        V((T, 4, 2, 80, 128), f32), V((T, 4, 80, 128), f32),
        V((T, 4, 80, 128), f32), V((T, 3, 80, 128), f32),
        V((T, n, 80, 128), bf16),
        D((3,)), D((4,)), D(()), D((T, 2)), D((T, 2)),
        D((2, T, 5)), D((2, T, 5)),
        D((T, 4)), D((T, 4)), D((T, 4)), D((T, 4)), D((T, 3)), D((T, 3)),
        D((T, n // 2 - 1)), D((T, n // 2 - 1)), D((T, n // 2)), D((T, n // 2)),
    ]
    vm = pl.BlockSpec(memory_space=pltpu.VMEM)
    hbm = pl.BlockSpec(memory_space=pl.ANY)
    factors, loadings, fit = pl.pallas_call(
        functools.partial(kernel, n),
        out_shape=(
            jax.ShapeDtypeStruct(cell_init.shape, f32),
            jax.ShapeDtypeStruct(load_init.shape, f32),
            jax.ShapeDtypeStruct((nb, 128), f32),
        ),
        in_specs=[hbm] * 5,
        out_specs=(vm, vm, vm),
        scratch_shapes=scratch,
        compiler_params=pltpu.CompilerParams(
            collective_id=0, has_side_effects=True, vmem_limit_bytes=48 * 1024 * 1024
        ),
    )(band_offsets, counts, cell_init, load_init, band_weights)
    return factors, loadings, fit.reshape(-1)


def extended(cells, sides, width):
    for axis, dim in sides:
        count = lax.axis_size(axis)
        ends = count - 1
        head = lax.slice_in_dim(cells, 0, width, axis=dim)
        tail = lax.slice_in_dim(cells, cells.shape[dim] - width, cells.shape[dim], axis=dim)
        cells = jnp.concatenate(
            [
                lax.ppermute(tail, axis, [(i, (i + 1) % count) for i in range(ends)]),
                cells,
                lax.ppermute(head, axis, [((i + 1) % count, i) for i in range(ends)]),
            ],
            axis=dim,
        )
    return cells


def make_gene_rows(counts, fact_half):
    return lax.dot_general(
        counts, fact_half, (((0,), (1,)), ((), ())), preferred_element_type=jnp.float32
    )


def body(counts, cell_init, load_init, band_offsets, band_weights):
    count = lax.axis_size("cell")
    if count == 16 and load_init.shape == (64, 160) and counts.shape[0] == 128 * band_weights.shape[0]:
        return fused(count, counts, cell_init, load_init, band_offsets, band_weights)
    highest = lax.Precision.HIGHEST
    factors = cell_init
    loadings = load_init
    rank = factors.shape[0]
    nblocks = band_weights.shape[0]
    block = band_weights.shape[-1]
    degree = jnp.sum(band_weights.astype(jnp.float32), axis=(1, 3)).reshape(-1)
    positions = jnp.arange(nblocks, dtype=jnp.int32)[:, None] + 2 + band_offsets
    load_half = loadings.astype(jnp.bfloat16)
    for sweep in range(ITERS):
        fact_half = factors.astype(jnp.bfloat16)
        local_gram = jnp.dot(factors, factors.T, precision=highest)
        own_sums = lax.psum_scatter(
            make_gene_rows(counts, fact_half), "cell", scatter_dimension=0, tiled=True
        )
        factor_gram = lax.psum(local_gram, "cell")
        loadings = (
            loadings * own_sums.T / (jnp.dot(factor_gram, loadings, precision=highest) + epsilon)
        )
        load_gram = lax.psum(jnp.dot(loadings, loadings.T, precision=highest), "cell")
        load_half = lax.all_gather(loadings.astype(jnp.bfloat16), "cell", axis=1, tiled=True)
        data_term = lax.dot_general(
            load_half, counts, (((1,), (1,)), ((), ())), preferred_element_type=jnp.float32
        )
        padded = extended(fact_half, (("cell", 1),), 2 * block)
        blocks = padded.reshape(rank, nblocks + 4, block)
        picked = jnp.take(blocks, positions, axis=1)
        result = jnp.einsum(
            "nsij,knsj->kni", band_weights, picked, preferred_element_type=jnp.float32
        )
        graph_term = result.reshape(rank, nblocks * block)
        numer = data_term + graph_weight * graph_term
        denom = (
            jnp.dot(load_gram, factors, precision=highest)
            + graph_weight * degree[None, :] * factors
            + epsilon
        )
        factors = factors * numer / denom
    fact_half = factors.astype(jnp.bfloat16)
    recon = lax.dot_general(
        fact_half, load_half, (((0,), (0,)), ((), ())), preferred_element_type=jnp.float32
    )
    fit_error = jnp.mean(jnp.square(counts.astype(jnp.float32) - recon), axis=1)
    return (factors, loadings, fit_error)


def solution(mesh):
    in_specs = (
        P(("grp", "cell"), None),
        P(None, ("grp", "cell")),
        P(None, ("grp", "cell")),
        P(("grp", "cell"), None),
        P(("grp", "cell"), None, None, None),
    )
    out_specs = (P(None, ("grp", "cell")), P(None, ("grp", "cell")), P(("grp", "cell")))
    return jax.shard_map(body, mesh=mesh, in_specs=in_specs, out_specs=out_specs, check_vma=False)
```
